256 devices in a mesh: ctx: 32 (over x, y, core), tp: 8 (over z).
Axes of the slice: x: 4, y: 4, z: 8, core: 2. Of those that a mesh axis runs over, the one named last changes fastest.
Arguments:
- queries: bfloat16 [16384, 4096], P('ctx', 'tp'), may hold values from -160 to 160, as said below
- key_head_rows: bfloat16 [16384, 1024], P('ctx', 'tp'), may hold values from -6 to 6
- values: bfloat16 [16384, 1024], P('ctx', 'tp'), may hold values from -6 to 6
- doc_lengths: int32 [1, 16], replicated, may hold values from 1 to 4096, 16384 in all within a row
- score_weight: bfloat16 [4096], P('tp'), may hold values from -0.375 to 0.375
Outputs:
- attended: bfloat16 [16384, 4096], P('ctx', 'tp')
- token_score: float32 [16384], P('ctx')
The draws below stay inside these ranges and needn't reach their ends.
Inputs may be any that keep to these rules, and one draw needn't show every extreme that they name: `queries`: hidden rows may hold large multiples of keys.
All inputs are finite; a program needn't handle non-finite values.
Results may differ from the reference program's by a relative error of at most 0.0045.
Values may be sent and summed in bfloat16 or wider, within the bound.
No kernel may reach another device: no remote copies, remote signals or barrier semaphores. Data moves between devices by JAX's collectives and lax.ppermute only.
A program may use at most 64 MiB of HBM per device.

```python
import math
import jax
import jax.numpy as jnp
import numpy as np
from jax import lax

HEAD_SIZE = 128
QUERY_HEADS = 32
KEY_VALUE_HEADS = 8
BLOCK_TOKENS = 128
DOC_MAX = 4096
NDOC = 16
TOKEN_TOTAL = 16384
SEQ = 16384
ROWS = 1


def shared_keys(key):
    start_offset = jax.random.normal(jax.random.fold_in(key, 101), (TOKEN_TOTAL, KEY_VALUE_HEADS * HEAD_SIZE), jnp.float32)
    return jnp.clip(start_offset, -6.0, 6.0)


def draw_key_head_rows(key, part):
    start_offset = shared_keys(key)
    return start_offset.astype(jnp.bfloat16)


def draw_queries(key, part):
    key = jax.random.fold_in(key, 2)
    first_key = jax.random.fold_in(key, 0)
    drawn = jnp.clip(jax.random.normal(first_key, (TOKEN_TOTAL, QUERY_HEADS * HEAD_SIZE), jnp.float32), -6.0, 6.0)
    return drawn.astype(jnp.bfloat16)


def levels(rng, shape, cuts, smallest, top_value):
    loudness = 1.0
    for position, shards_of in cuts:
        steps = jax.random.uniform(jax.random.fold_in(jax.random.fold_in(rng, 6), position), (shards_of,), jnp.float32, smallest / len(cuts), top_value / len(cuts))
        loudness = loudness * jnp.repeat(jnp.exp(steps), shape[position] // shards_of).reshape((-1,) + (1,) * (len(shape) - 1 - position))
    return loudness


def length_profile(count, total, most, lean):
    portions = [(1 << 20) // math.isqrt(standing ** lean) + 1 for standing in range(2, count + 1)]
    rest, given = total - most - (count - 1), [1] * (count - 1)
    while rest > 0:
        candidates = [i for i in range(count - 1) if given[i] < most]
        whole, budget = sum([portions[i] for i in candidates]), rest
        for i in candidates:
            addition = min(most - given[i], max(1, budget * portions[i] // whole), rest)
            given[i] = given[i] + addition
            rest = rest - addition
    return np.array([most] + given)


def uneven_parts(own_key, number_of, total, limit, lean):
    if number_of == 2:
        one = jax.random.randint(own_key, (), max(1, total - limit), min(limit, total - 1) + 1)
        return jnp.stack([one, total - one])
    sizes = jnp.asarray(length_profile(number_of, total, limit, lean), jnp.int32)
    twos = (number_of - 1) // 2
    donor, receiver = sizes[1:1 + 2 * twos:2], sizes[2:2 + 2 * twos:2]
    margin = jnp.minimum(donor - 1, limit - receiver)
    passed = jax.random.randint(jax.random.fold_in(own_key, 1), (twos,), 0, 1 << 20) % (margin + 1)
    sizes = sizes.at[1:1 + 2 * twos:2].set(donor - passed).at[2:2 + 2 * twos:2].set(receiver + passed)
    return sizes[jax.random.permutation(jax.random.fold_in(own_key, 2), number_of)]


def bell_draw(own_key, extent, width, limit, cuts=(), kind=jnp.bfloat16):
    loudness = levels(own_key, extent, cuts, -0.22, 0.18) if cuts else 1.0
    values = jax.random.normal(own_key, extent, jnp.float32) * width * loudness
    return jnp.minimum(jnp.maximum(values, -limit), limit).astype(kind)


def setup_inputs(seed: int = 0) -> dict:
    seeds = jax.random.split(jax.random.key(seed), 6)
    queries = draw_queries(jax.random.fold_in(seeds[5], 71), 0)
    key_head_rows = draw_key_head_rows(jax.random.fold_in(seeds[5], 71), 0)
    values = bell_draw(seeds[2], (TOKEN_TOTAL, KEY_VALUE_HEADS * HEAD_SIZE), 1.0, 6.0, ((0, 32), (1, 8)))
    doc_lengths = jax.vmap(lambda own: uneven_parts(own, NDOC, SEQ, DOC_MAX, 2))(jax.random.split(seeds[3], ROWS)).reshape((ROWS, NDOC)).astype(jnp.int32)
    score_weight = bell_draw(seeds[4], (QUERY_HEADS * HEAD_SIZE,), (QUERY_HEADS * HEAD_SIZE // 16) ** -0.5, 0.375, ((0, 8),))
    return dict(queries=queries, key_head_rows=key_head_rows, values=values, doc_lengths=doc_lengths, score_weight=score_weight)


def doc_start_table(doc_lengths):
    offsets = (jnp.cumsum(doc_lengths, axis=1) - doc_lengths).astype(jnp.int32)
    row_first = (jnp.arange(doc_lengths.shape[0], dtype=jnp.int32) * SEQ)[:, None]
    return (row_first + offsets).reshape(-1).astype(jnp.int32)

def doc_starts(positions, doc_table):
    below = doc_table[None, :] <= positions[:, None]
    return lax.optimization_barrier(jnp.max(jnp.where(below, doc_table[None, :], 0), axis=1)).astype(jnp.int32)

def reference(queries, key_head_rows, values, doc_lengths, score_weight):
    group_width = QUERY_HEADS // KEY_VALUE_HEADS
    total_tokens = queries.shape[0]
    block_total = total_tokens // BLOCK_TOKENS
    visible_span = ((DOC_MAX + BLOCK_TOKENS - 1) // BLOCK_TOKENS + 1) * BLOCK_TOKENS
    leading_rows = visible_span - BLOCK_TOKENS
    doc_table = doc_start_table(doc_lengths)
    padded_keys = jnp.concatenate([jnp.zeros((leading_rows, KEY_VALUE_HEADS * HEAD_SIZE), key_head_rows.dtype), key_head_rows], axis=0)
    padded_values = jnp.concatenate([jnp.zeros((leading_rows, KEY_VALUE_HEADS * HEAD_SIZE), values.dtype), values], axis=0)
    score_scale = 1.0 / math.sqrt(HEAD_SIZE)

    def attend_block(block_index):
        leading_token = (block_index * BLOCK_TOKENS).astype(jnp.int32)
        index_zero = jnp.int32(0)
        block_query_rows = lax.dynamic_slice(queries, (leading_token, index_zero), (BLOCK_TOKENS, QUERY_HEADS * HEAD_SIZE))
        block_query_rows = block_query_rows.astype(jnp.float32).reshape(BLOCK_TOKENS, KEY_VALUE_HEADS, group_width, HEAD_SIZE)
        block_keys = lax.dynamic_slice(padded_keys, (leading_token, index_zero), (visible_span, KEY_VALUE_HEADS * HEAD_SIZE))
        block_keys = block_keys.astype(jnp.float32).reshape(visible_span, KEY_VALUE_HEADS, HEAD_SIZE)
        block_values = lax.dynamic_slice(padded_values, (leading_token, index_zero), (visible_span, KEY_VALUE_HEADS * HEAD_SIZE))
        block_values = block_values.astype(jnp.float32).reshape(visible_span, KEY_VALUE_HEADS, HEAD_SIZE)
        positions = leading_token + jnp.arange(BLOCK_TOKENS, dtype=jnp.int32)
        key_pos = leading_token - leading_rows + jnp.arange(visible_span, dtype=jnp.int32)
        starts = doc_starts(positions, doc_table)
        allowed = (key_pos[None, :] >= starts[:, None]) & (key_pos[None, :] <= positions[:, None])
        scores = jnp.einsum('tkgd,ukd->tkgu', block_query_rows, block_keys) * score_scale
        scores = jnp.where(allowed[:, None, None, :], scores, -jnp.inf)
        row_max = lax.optimization_barrier(jnp.max(scores, axis=-1, keepdims=True))
        weights = jnp.exp(scores - row_max)
        denominator = lax.optimization_barrier(jnp.sum(weights, axis=-1))
        rounded = lax.optimization_barrier(weights.astype(jnp.bfloat16)).astype(jnp.float32)
        mixed = jnp.einsum('tkgu,ukd->tkgd', rounded, block_values) / denominator[..., None]
        return mixed.reshape(BLOCK_TOKENS, QUERY_HEADS * HEAD_SIZE).astype(jnp.bfloat16)
    attended = lax.map(attend_block, jnp.arange(block_total, dtype=jnp.int32))
    attended = attended.reshape(total_tokens, QUERY_HEADS * HEAD_SIZE)
    token_score = jnp.dot(attended, score_weight, preferred_element_type=jnp.float32)
    return (attended, token_score)
```

```python
import functools
import math

import jax, jax.numpy as jnp
from jax import lax
from jax.experimental import pallas as pl
from jax.experimental.pallas import tpu as pltpu
from jax.sharding import PartitionSpec as P
C=math.log2(math.e)/math.sqrt(128)
NEG=-1e30
F32=jnp.float32; BF=jnp.bfloat16
T=512; QB=128; G=4; R=512; NQ=4; D=128; AR=144
def offsets(doc_ref, idx):
    off=jnp.int32(0); out=jnp.full(idx.shape,1<<29,jnp.int32)
    for d in range(16):
        out=jnp.where(idx==d,off,out)
        off=off+doc_ref[0,d]
    return out
def first_kernel(get_me, doc_ref, q_ref, kv_ref, qt_ref, m_ref, acc_ref, s0, s1):
    me=get_me(); base=me*T
    offc=offsets(doc_ref,lax.broadcasted_iota(jnp.int32,(D,1),0))
    nxt=offsets(doc_ref,lax.broadcasted_iota(jnp.int32,(D,1),0)+1)
    nxt=jnp.where(nxt==(1<<29),1<<28,nxt)
    kk=kv_ref[:,:D]
    va=jnp.concatenate([kv_ref[:,D:].T,jnp.ones((AR-D,T),BF)],0)
    sl=(s0,s1); mxs={}; pos={}
    def prep(qb):
        p=base+qb*QB+lax.broadcasted_iota(jnp.int32,(1,QB),1)
        inside=(p>=offc)&(p<nxt)
        ex=jnp.where(inside,NEG,0.0).astype(BF)
        for h in range(G):
            qt_ref[qb*256:qb*256+D,h*D:(h+1)*D]=q_ref[qb*QB:(qb+1)*QB,h*D:(h+1)*D].T
            qt_ref[qb*256+D:qb*256+2*D,h*D:(h+1)*D]=ex
        st=jnp.sum(jnp.where(inside,offc,0),axis=0,keepdims=True)
        return p,st
    def A(qb,slot):
        p,st=prep(qb)
        n=(qb+1)*QB
        kp=base+lax.broadcasted_iota(jnp.int32,(n,QB),0)
        bias=jnp.where((kp>=st)&(kp<=p),0.0,NEG)
        s=jnp.dot(kk[:n],qt_ref[qb*256:qb*256+D,:],preferred_element_type=F32)+jnp.concatenate([bias]*G,1)
        sl[slot][:n]=s
        mxs[qb]=jnp.max(s,axis=0,keepdims=True)
    def B(qb,slot):
        n=(qb+1)*QB
        mn=mxs[qb]
        p=jnp.exp2((sl[slot][:n]-mn)*C).astype(BF)
        acc_ref[qb*AR:(qb+1)*AR,:]=jnp.dot(va[:,:n],p,preferred_element_type=F32)
        m_ref[qb*8:(qb+1)*8,:]=jnp.broadcast_to(mn,(8,R))
    A(0,0)
    for qb in range(NQ):
        if qb+1<NQ: A(qb+1,(qb+1)%2)
        B(qb,qb%2)
def step_kernel(get_me, chunks, final, loop, doc_ref, qt_ref, m_ref, acc_ref, *refs):
    n=len(chunks)
    kv=refs[:n]; refs=refs[n:]
    if final:
        w_ref,out_ref,part_ref=refs[:3]; refs=refs[3:]
    else:
        mo_ref,ao_ref=refs[:2]; refs=refs[2:]
    s0,s1,ka,va=refs
    me=get_me()
    offr=offsets(doc_ref,lax.broadcasted_iota(jnp.int32,(1,D),1))
    for c,(k,other) in enumerate(chunks):
        src=me-2*k if not other else me+1-2*(me%2)-2*k
        u0=src*T
        if other and k==0: u0=jnp.where(me%2==0,-(1<<24),u0)
        u=u0+lax.broadcasted_iota(jnp.int32,(T,1),0)
        ka[c*T:(c+1)*T,:D]=kv[c][:,:D]
        ka[c*T:(c+1)*T,D:]=jnp.where(u<offr,1.0,0.0).astype(BF)
        va[:D,c*T:(c+1)*T]=kv[c][:,D:].T
    va[D:,:]=jnp.ones((AR-D,n*T),BF)
    sl=(s0,s1)
    def A(qb,slot):
        mx=None
        for c in range(n):
            s=jnp.dot(ka[c*T:(c+1)*T,:],qt_ref[pl.ds(qb*256,256),:],preferred_element_type=F32)
            sl[slot][c*T:(c+1)*T,:]=s
            x=jnp.max(s.reshape(T//8,8,R),axis=0)
            mx=x if mx is None else jnp.maximum(mx,x)
        return jnp.max(mx,axis=0,keepdims=True)
    def B(qb,slot,mx):
        m=m_ref[pl.ds(qb*8,8),:][:1]
        mn=jnp.maximum(m,mx)
        a=jnp.exp2((m-mn)*C)
        o=acc_ref[pl.ds(qb*AR,AR),:]*a
        for c in range(n):
            p=jnp.exp2((sl[slot][c*T:(c+1)*T,:]-mn)*C).astype(BF)
            o=o+jnp.dot(va[:,c*T:(c+1)*T],p,preferred_element_type=F32)
        if not final:
            ao_ref[pl.ds(qb*AR,AR),:]=o
            mo_ref[pl.ds(qb*8,8),:]=jnp.broadcast_to(mn,(8,R))
        else:
            o=o[:D]*(1.0/o[D:D+1])
            tot=jnp.zeros((16,QB),F32)
            for h in range(G):
                oh=o[:,h*D:(h+1)*D].T.astype(BF)
                out_ref[pl.ds(qb*QB,QB),h*D:(h+1)*D]=oh
                wh=jnp.broadcast_to(w_ref[:,h*D:(h+1)*D],(16,D))
                tot=tot+lax.dot_general(wh,oh,(((1,),(1,)),((),())),preferred_element_type=F32)
            part_ref[:,pl.ds(qb*QB,QB)]=tot[:8]
    if loop:
        mx=A(0,0)
        def bd(j,mx0):
            mx1=A(2*j+1,1)
            B(2*j,0,mx0)
            mx2=A(jnp.minimum(2*j+2,NQ-1),0)
            B(2*j+1,1,mx1)
            return mx2
        lax.fori_loop(0,NQ//2,bd,mx)
    else:
        mx=A(0,0)
        for qb in range(NQ):
            if qb+1<NQ: mx2=A(qb+1,(qb+1)%2)
            B(qb,qb%2,mx)
            mx=mx2
SD = jax.ShapeDtypeStruct
V=pl.BlockSpec(memory_space=pltpu.VMEM); SM=pl.BlockSpec(memory_space=pltpu.SMEM)
def first(get_me,doc,q,kv):
    return pl.pallas_call(functools.partial(first_kernel,get_me),out_shape=(SD((NQ*256,R),BF),SD((NQ*8,R),F32),SD((NQ*AR,R),F32)),
      in_specs=[SM,V,V],out_specs=(V,V,V),scratch_shapes=[pltpu.VMEM((T,R),F32)]*2,compiler_params=pltpu.CompilerParams(vmem_limit_bytes=32<<20),name="att_first")(doc,q,kv)
def step(get_me,chunks,doc,st,kvs,w=None,loop=True):
    n=len(chunks); final=w is not None
    outs=(SD((T,512),BF),SD((8,T),F32)) if final else (SD((NQ*8,R),F32),SD((NQ*AR,R),F32))
    qt,m,acc=st
    args=[doc,qt,m,acc,*kvs]+([w] if final else [])
    r=pl.pallas_call(functools.partial(step_kernel,get_me,chunks,final,loop),out_shape=outs,in_specs=[SM]+[V]*(len(args)-1),out_specs=(V,V),
      scratch_shapes=[pltpu.VMEM((n*T,R),F32)]*2+[pltpu.VMEM((n*T,2*D),BF),pltpu.VMEM((AR,n*T),BF)],compiler_params=pltpu.CompilerParams(vmem_limit_bytes=40<<20),
      name="att_final" if final else "att_step")(*args)
    return r if final else (qt,)+tuple(r)


def shards(queries, key_head_rows, values, doc_lengths, score_weight):
    ctx = lax.axis_size("ctx")
    kv = jnp.concatenate([key_head_rows, values], axis=1)

    def shift(x, by):
        return lax.ppermute(x, "ctx", [(i, (i + by) % ctx) for i in range(ctx)])

    def swap(x):
        return lax.ppermute(x, "ctx", [(i, i ^ 1) for i in range(ctx)])

    same = {0: kv}
    for k in (4, 1, 3, 2):
        same[k] = shift(kv, 2 * k)
    other = {k: swap(same[k]) for k in (0, 4, 1, 3, 2)}

    def take(chunks):
        return [other[k] if o else same[k] for k, o in chunks]

    me = functools.partial(lax.axis_index, "ctx")
    state = first(me, doc_lengths, queries, kv)
    near = [(0, 1), (1, 0), (1, 1)]
    far = [(4, 0), (4, 1)]
    rest = [(2, 0), (2, 1), (3, 0), (3, 1)]
    state = step(me, near, doc_lengths, state, take(near))
    state = step(me, far, doc_lengths, state, take(far))
    attended, part = step(me, rest, doc_lengths, state, take(rest), score_weight.reshape(1, -1))
    parts = lax.all_to_all(part, "tp", 0, 0, tiled=True)
    return attended, jnp.sum(parts, axis=0)


def solution(mesh):
    return jax.shard_map(
        shards,
        mesh=mesh,
        in_specs=(P("ctx", "tp"), P("ctx", "tp"), P("ctx", "tp"), P(), P("tp")),
        out_specs=(P("ctx", "tp"), P("ctx")),
        check_vma=False,
    )
```

```python
import functools
import math

import jax
import jax.numpy as jnp
from jax import lax
from jax.experimental import pallas as pl
from jax.experimental.pallas import tpu as pltpu
from jax.sharding import PartitionSpec as P
from jax.sharding import PartitionSpec as P

D = 128
T = 512
QB = 128
G = 4
R = QB * G
NQ = T // QB
AR = D + 16
NDOC = 16
BK = 256
FAR = 1 << 28
C = math.log2(math.e) / math.sqrt(D)
NEG = -1e30
F32 = jnp.float32
BF = jnp.bfloat16
SD = jax.ShapeDtypeStruct
VM = pl.BlockSpec(memory_space=pltpu.VMEM)
TOKEN = SD((16, 128), BF)
ANY = pl.BlockSpec(memory_space=pl.ANY)
SM = pl.BlockSpec(memory_space=pltpu.SMEM)


def offsets(doc_ref, index):
    start = jnp.int32(0)
    out = jnp.full(index.shape, FAR, jnp.int32)
    for d in range(NDOC):
        out = jnp.where(index == d, start, out)
        start = start + doc_ref[0, d]
    return out


def prep_kernel(k_ref, v_ref, kv_ref, held, sems):
    values = pltpu.make_async_copy(v_ref, held, sems.at[0])
    keys = pltpu.make_async_copy(k_ref, kv_ref.at[:, :D], sems.at[1])
    values.start()
    keys.start()
    values.wait()
    for i in range(T // D):
        rows = slice(i * D, (i + 1) * D)
        kv_ref[rows, D:] = held[rows, :].T
    keys.wait()


def value_rows(kv_ref):
    blocks = [kv_ref[i * D : (i + 1) * D, D:] for i in range(T // D)]
    return jnp.concatenate(
        [jnp.concatenate(blocks, 1), jnp.ones((AR - D, T), BF)], 0
    )


def first_kernel(get_me, doc_ref, q_ref, kv_ref, qt_ref, m_ref, acc_ref, token_ref, s0, s1):
    base = get_me() * T
    ids = lax.broadcasted_iota(jnp.int32, (D, 1), 0)
    begin = offsets(doc_ref, ids)
    end = jnp.where(ids == NDOC - 1, FAR, offsets(doc_ref, ids + 1))
    va = value_rows(kv_ref)
    held = (s0, s1)
    tops = {}

    def scores(qb):
        pos = base + qb * QB + lax.broadcasted_iota(jnp.int32, (1, QB), 1)
        inside = (pos >= begin) & (pos < end)
        for h in range(G):
            cols = slice(h * D, (h + 1) * D)
            qt_ref[qb * 2 * D : qb * 2 * D + D, cols] = q_ref[qb * QB : (qb + 1) * QB, cols].T
            qt_ref[qb * 2 * D + D : (qb + 1) * 2 * D, cols] = jnp.where(inside, NEG, 0.0).astype(BF)
        start = jnp.sum(jnp.where(inside, begin, 0), axis=0, keepdims=True)
        n = (qb + 1) * QB
        key = base + lax.broadcasted_iota(jnp.int32, (n, QB), 0)
        bias = jnp.where((key >= start) & (key <= pos), 0.0, NEG)
        s = jnp.dot(kv_ref[:n, :D], qt_ref[qb * 2 * D : qb * 2 * D + D, :], preferred_element_type=F32)
        s = s + jnp.concatenate([bias] * G, 1)
        held[qb % 2][:n] = s
        tops[qb] = jnp.max(s, axis=0, keepdims=True)

    token_ref[...] = jnp.zeros_like(token_ref)
    scores(0)
    for qb in range(NQ):
        if qb + 1 < NQ:
            scores(qb + 1)
        n = (qb + 1) * QB
        p = jnp.exp2((held[qb % 2][:n] - tops[qb]) * C).astype(BF)
        acc_ref[qb * AR : (qb + 1) * AR, :] = jnp.dot(va[:, :n], p, preferred_element_type=F32)
        m_ref[qb * 8 : (qb + 1) * 8, :] = jnp.broadcast_to(tops[qb], (8, R))


def step_kernel(get_me, chunks, final, doc_ref, qt_ref, m_ref, acc_ref, *refs):
    n = len(chunks)
    me = get_me()
    core = lax.rem(me, 2)
    offs = offsets(doc_ref, lax.broadcasted_iota(jnp.int32, (1, D), 1))
    kv = list(refs[: sum(len(c) for c in chunks)])
    refs = refs[len(kv) :]
    if final:
        w_ref, out_ref, part_ref = refs[:3]
        refs = refs[3:]
    else:
        mo_ref, ao_ref, token_ref = refs[:3]
        refs = refs[3:]
        token_ref[...] = jnp.zeros_like(token_ref)
    s0, s1, p0, p1, ka, va = refs
    held, probs = (s0, s1), (p0, p1)

    def load(c, piece, ref):
        k, other = piece
        src = (me + 1 - 2 * core if other else me) - 2 * k
        key = src * T + lax.broadcasted_iota(jnp.int32, (T, 1), 0)
        rows = slice(c * T, (c + 1) * T)
        ka[rows, :D] = ref[:, :D]
        ka[rows, D:] = jnp.where(key < offs, 1.0, 0.0).astype(BF)
        va[:, rows] = value_rows(ref)

    for c, pieces in enumerate(chunks):
        if len(pieces) == 1:
            load(c, pieces[0], kv.pop(0))
        else:
            for which, piece in enumerate(pieces):
                pl.when(core == which)(functools.partial(load, c, piece, kv.pop(0)))

    prior, top = {}, {}

    def set_top(qb, mx):
        prior[qb] = m_ref[qb * 8 : qb * 8 + 1, :]
        top[qb] = jnp.maximum(prior[qb], jnp.max(mx, axis=0, keepdims=True))

    def finish(qb, o):
        o = acc_ref[qb * AR : (qb + 1) * AR, :] * jnp.exp2((prior[qb] - top[qb]) * C) + o
        if not final:
            ao_ref[qb * AR : (qb + 1) * AR, :] = o
            mo_ref[qb * 8 : qb * 8 + 8, :] = jnp.broadcast_to(top[qb], (8, R))
            return
        ob = (o[:D] * (1.0 / o[D : D + 1])).astype(BF)
        for h in range(G):
            cols = slice(h * D, (h + 1) * D)
            out_ref[qb * QB : (qb + 1) * QB, cols] = ob[:, cols].T
        heads = jnp.dot(w_ref[...], ob, preferred_element_type=F32)
        score = sum(heads[h : h + 1, h * D : (h + 1) * D] for h in range(G))
        for z in range(8):
            part_ref[z * 8 + qb : z * 8 + qb + 1, :] = score

    if final:
        part_ref[...] = jnp.zeros_like(part_ref)
    for qb in range(-1, NQ + 1):
        mx = o = None
        for j in range(n * T // BK):
            rows = slice(j * BK, (j + 1) * BK)
            if qb + 1 < NQ:
                s = jnp.dot(ka[rows, :], qt_ref[(qb + 1) * 2 * D : (qb + 2) * 2 * D, :], preferred_element_type=F32)
                held[(qb + 1) % 2][rows, :] = s
                x = jnp.max(s.reshape(BK // 8, 8, R), axis=0)
                mx = x if mx is None else jnp.maximum(mx, x)
            if 0 <= qb < NQ:
                probs[qb % 2][rows, :] = jnp.exp2((held[qb % 2][rows, :] - top[qb]) * C).astype(BF)
            if qb >= 1:
                x = jnp.dot(va[:, rows], probs[(qb - 1) % 2][rows, :], preferred_element_type=F32)
                o = x if o is None else o + x
        if qb + 1 < NQ:
            set_top(qb + 1, mx)
        if qb >= 1:
            finish(qb - 1, o)


def call(kernel, name, out, specs, scratch, flops, vmem=36):
    return pl.pallas_call(
        kernel,
        out_shape=out,
        in_specs=specs,
        out_specs=jax.tree.map(lambda _: VM, out),
        scratch_shapes=scratch,
        name=name,
        cost_estimate=pl.CostEstimate(flops=flops, bytes_accessed=1 << 20, transcendentals=0),
        compiler_params=pltpu.CompilerParams(vmem_limit_bytes=vmem << 20),
    )


def after_kernel(x_ref, token_ref, out_ref):
    out_ref[...] = x_ref[...]


def after(x, token):
    return call(after_kernel, "after", SD(x.shape, x.dtype), [VM, VM], [], 1 << 20)(x, token)


def prep(k, v):
    scratch = [pltpu.VMEM((T, D), BF), pltpu.SemaphoreType.DMA((2,))]
    return call(prep_kernel, "prep", SD((T, 2 * D), BF), [ANY, ANY], scratch, 1 << 20, 60)(k, v)


def first(get_me, doc, q, kv):
    out = (SD((NQ * 2 * D, R), BF), SD((NQ * 8, R), F32), SD((NQ * AR, R), F32), TOKEN)
    kernel = functools.partial(first_kernel, get_me)
    return call(kernel, "att_first", out, [SM, VM, VM], [pltpu.VMEM((T, R), F32)] * 2, 1 << 31)(doc, q, kv)


def step(get_me, chunks, doc, state, kvs, w=None):
    n = len(chunks)
    final = w is not None
    out = (SD((T, G * D), BF), SD((64, QB), F32)) if final else (SD((NQ * 8, R), F32), SD((NQ * AR, R), F32), TOKEN)
    args = [doc, *state[:3], *kvs] + ([w] if final else [])
    scratch = (
        [pltpu.VMEM((n * T, R), F32)] * 2
        + [pltpu.VMEM((n * T, R), BF)] * 2
        + [pltpu.VMEM((n * T, 2 * D), BF), pltpu.VMEM((AR, n * T), BF)]
    )
    kernel = functools.partial(step_kernel, get_me, chunks, final)
    res = call(kernel, "att_final" if final else "att_step", out, [SM] + [VM] * (len(args) - 1), scratch, n << 31)(*args)
    return res if final else (state[0], *res)


CALLS = [
    [[(4, 0)], [(1, 0)]],
    [[(4, 1), (0, 1)], [(1, 1)]],
    [[(3, 0)], [(3, 1)], [(2, 0)]],
    [[(2, 1)]],
]


def shards(queries, key_head_rows, values, doc_lengths, score_weight):
    ctx = lax.axis_size("ctx")
    kv = prep(key_head_rows, values)

    def shift(x, by):
        return lax.ppermute(x, "ctx", [(i, (i + by) % ctx) for i in range(ctx)])

    def swap(x):
        return lax.ppermute(x, "ctx", [(i, i ^ 1) for i in range(ctx)])

    def take(chunks):
        return [other[k] if o else same[k] for pieces in chunks for k, o in pieces]

    me = functools.partial(lax.axis_index, "ctx")
    weights = jnp.pad(score_weight.reshape(G, D), ((0, 16 - G), (0, 0)))
    same = {4: shift(kv, 8), 1: shift(kv, 2)}
    other = {0: swap(kv)}
    state = first(me, doc_lengths, queries, kv)
    for k, far, by in ((4, 3, -2), (1, 2, 2)):
        same[k] = after(same[k], state[3])
        same[far] = shift(same[k], by)
        other[k] = swap(same[k])
    for chunks in CALLS[:2]:
        state = step(me, chunks, doc_lengths, state, take(chunks))
    for k in (3, 2):
        same[k] = after(same[k], state[3])
        other[k] = swap(same[k])
    state = step(me, CALLS[2], doc_lengths, state, take(CALLS[2]))
    attended, part = step(me, CALLS[3], doc_lengths, state, take(CALLS[3]), weights)
    parts = lax.all_to_all(part, "tp", 0, 0, tiled=True)
    score = jnp.sum(parts.reshape(8, 8, QB), axis=0)[:NQ]
    return attended, score.reshape(T)


def solution(mesh):
    return jax.shard_map(
        shards,
        mesh=mesh,
        in_specs=(P("ctx", "tp"), P("ctx", "tp"), P("ctx", "tp"), P(), P("tp")),
        out_specs=(P("ctx", "tp"), P("ctx")),
        check_vma=False,
    )
```

```python
import functools
import math

import jax
import jax.numpy as jnp
from jax import lax
from jax.experimental import pallas as pl
from jax.experimental.pallas import tpu as pltpu
from jax.sharding import PartitionSpec as P

D = 128
T = 512
QB = 128
G = 4
R = QB * G
NQ = T // QB
AR = D + 16
TOP = D + 8
NDOC = 16
BK = 256
FAR = 1 << 28
C = math.log2(math.e) / math.sqrt(D)
NEG = -1e30
F32 = jnp.float32
BF = jnp.bfloat16
SD = jax.ShapeDtypeStruct
VM = pl.BlockSpec(memory_space=pltpu.VMEM)
TOKEN = SD((16, 128), BF)
ANY = pl.BlockSpec(memory_space=pl.ANY)
SM = pl.BlockSpec(memory_space=pltpu.SMEM)


def offsets(doc_ref, index):
    start = jnp.int32(0)
    out = jnp.full(index.shape, FAR, jnp.int32)
    for d in range(NDOC):
        out = jnp.where(index == d, start, out)
        start = start + doc_ref[0, d]
    return out


def prep_kernel(k_ref, v_ref, q_ref, kv_ref, q_out, held, sems):
    values = pltpu.make_async_copy(v_ref, held, sems.at[0])
    keys = pltpu.make_async_copy(k_ref, kv_ref.at[:, :D], sems.at[1])
    queries = pltpu.make_async_copy(q_ref, q_out, sems.at[2])
    values.start()
    keys.start()
    queries.start()
    values.wait()
    for i in range(T // D):
        rows = slice(i * D, (i + 1) * D)
        kv_ref[rows, D:] = held[rows, :].T
    keys.wait()
    queries.wait()


def value_rows(kv_ref):
    blocks = [kv_ref[i * D : (i + 1) * D, D:] for i in range(T // D)]
    return jnp.concatenate(
        [jnp.concatenate(blocks, 1), jnp.ones((AR - D, T), BF)], 0
    )


def first_kernel(get_me, doc_ref, q_ref, far_q_ref, kv_ref, qt_ref, st_ref, token_ref, s0, s1):
    me = get_me()
    other = me + 1 - 2 * lax.rem(me, 2)
    ids = lax.broadcasted_iota(jnp.int32, (D, 1), 0)
    begin = offsets(doc_ref, ids)
    end = jnp.where(ids == NDOC - 1, FAR, offsets(doc_ref, ids + 1))
    va = value_rows(kv_ref)
    held = (s0, s1)
    tops = {}

    def turn(src, base, qb, row):
        pos = base + qb * QB + lax.broadcasted_iota(jnp.int32, (1, QB), 1)
        inside = (pos >= begin) & (pos < end)
        for h in range(G):
            cols = slice(h * D, (h + 1) * D)
            qt_ref[row : row + D, cols] = src[qb * QB : (qb + 1) * QB, cols].T
            qt_ref[row + D : row + 2 * D, cols] = jnp.where(inside, NEG, 0.0).astype(BF)
        return pos, jnp.sum(jnp.where(inside, begin, 0), axis=0, keepdims=True)

    def scores(qb):
        row = qb * 2 * D
        pos, start = turn(q_ref, me * T, qb, row)
        n = (qb + 1) * QB
        key = me * T + lax.broadcasted_iota(jnp.int32, (n, QB), 0)
        bias = jnp.where((key >= start) & (key <= pos), 0.0, NEG)
        s = jnp.dot(kv_ref[:n, :D], qt_ref[row : row + D, :], preferred_element_type=F32)
        s = s + jnp.concatenate([bias] * G, 1)
        held[qb % 2][:n] = s
        tops[qb] = jnp.max(s, axis=0, keepdims=True)

    token_ref[...] = jnp.zeros_like(token_ref)
    scores(0)
    for qb in range(NQ):
        if qb + 1 < NQ:
            scores(qb + 1)
        n = (qb + 1) * QB
        p = jnp.exp2((held[qb % 2][:n] - tops[qb]) * C).astype(BF)
        o = jnp.dot(va[:, :n], p, preferred_element_type=F32)
        put_state(st_ref, qb, o, tops[qb])
    for qb in range(NQ):
        turn(far_q_ref, other * T, qb, (NQ + qb) * 2 * D)


def put_state(st_ref, qb, o, top):
    st_ref[qb * AR : qb * AR + TOP, :] = o[:TOP]
    st_ref[qb * AR + TOP : (qb + 1) * AR, :] = jnp.broadcast_to(top, (AR - TOP, R))


def get_state(st_ref, qb):
    return st_ref[qb * AR : qb * AR + TOP, :], st_ref[qb * AR + TOP : qb * AR + TOP + 1, :]


def step_kernel(get_me, loads, items, doc_ref, qt_ref, st_ref, *refs):
    me = get_me()
    core = lax.rem(me, 2)
    offs = offsets(doc_ref, lax.broadcasted_iota(jnp.int32, (1, D), 1))
    kv = refs[:-8]
    out_ref, token_ref, s0, s1, p0, p1, ka, va = refs[-8:]
    held, probs = (s0, s1), (p0, p1)
    token_ref[...] = jnp.zeros_like(token_ref)

    def load(slot, which, back):
        key = (me - 2 * back) * T + lax.broadcasted_iota(jnp.int32, (T, 1), 0)
        rows = slice(slot * T, (slot + 1) * T)
        ka[rows, :D] = kv[which][:, :D]
        ka[rows, D:] = jnp.where(key < offs, 1.0, 0.0).astype(BF)
        va[:, rows] = value_rows(kv[which])

    for slot, (even, odd) in enumerate(loads):
        if even == odd:
            load(slot, *even)
        else:
            pl.when(core == 0)(functools.partial(load, slot, *even))
            pl.when(core == 1)(functools.partial(load, slot, *odd))

    top = {}
    count = len(items)
    for i in range(-1, count + 1):
        mx = o = None
        blocks = max(x[3] for x in items) * T // BK
        for j in range(blocks):
            rows = slice(j * BK, (j + 1) * BK)
            if i + 1 < count:
                qb, _, slot, _ = items[i + 1]
                s = jnp.dot(
                    ka[slot * T + j * BK : slot * T + (j + 1) * BK, :],
                    qt_ref[qb * 2 * D : (qb + 1) * 2 * D, :],
                    preferred_element_type=F32,
                )
                held[(i + 1) % 2][rows, :] = s
                x = jnp.max(s.reshape(BK // 8, 8, R), axis=0)
                mx = x if mx is None else jnp.maximum(mx, x)
            if 0 <= i < count:
                probs[i % 2][rows, :] = jnp.exp2((held[i % 2][rows, :] - top[i]) * C).astype(BF)
            if i >= 1:
                slot = items[i - 1][2]
                x = jnp.dot(
                    va[:, slot * T + j * BK : slot * T + (j + 1) * BK],
                    probs[(i - 1) % 2][rows, :],
                    preferred_element_type=F32,
                )
                o = x if o is None else o + x
        if i + 1 < count:
            top[i + 1] = jnp.max(mx, axis=0, keepdims=True)
            if items[i + 1][1] is not None:
                top[i + 1] = jnp.maximum(top[i + 1], get_state(st_ref, items[i + 1][1])[1])
        if i >= 1:
            o = o[:TOP]
            if items[i - 1][1] is not None:
                before, prior = get_state(st_ref, items[i - 1][1])
                o = before * jnp.exp2((prior - top[i - 1]) * C) + o
            put_state(out_ref, i - 1, o, top[i - 1])


def merge_kernel(mine_ref, theirs_ref, w_ref, out_ref, part_ref):
    part_ref[...] = jnp.zeros_like(part_ref)
    for qb in range(NQ):
        a, a_top = get_state(mine_ref, qb)
        b, b_top = get_state(theirs_ref, qb)
        top = jnp.maximum(a_top, b_top)
        o = a * jnp.exp2((a_top - top) * C) + b * jnp.exp2((b_top - top) * C)
        ob = (o[:D] * (1.0 / o[D : D + 1])).astype(BF)
        for h in range(G):
            cols = slice(h * D, (h + 1) * D)
            out_ref[qb * QB : (qb + 1) * QB, cols] = ob[:, cols].T
        heads = jnp.dot(w_ref[...], ob, preferred_element_type=F32)
        score = sum(heads[h : h + 1, h * D : (h + 1) * D] for h in range(G))
        for z in range(8):
            part_ref[z * 8 + qb : z * 8 + qb + 1, :] = score


def call(kernel, name, out, specs, scratch, flops, vmem=36):
    return pl.pallas_call(
        kernel,
        out_shape=out,
        in_specs=specs,
        out_specs=jax.tree.map(lambda _: VM, out),
        scratch_shapes=scratch,
        name=name,
        cost_estimate=pl.CostEstimate(flops=flops, bytes_accessed=1 << 20, transcendentals=0),
        compiler_params=pltpu.CompilerParams(vmem_limit_bytes=vmem << 20),
    )


def after_kernel(x_ref, token_ref, out_ref):
    out_ref[...] = x_ref[...]


def after(x, token):
    return call(after_kernel, "after", SD(x.shape, x.dtype), [VM, VM], [], 1 << 20)(x, token)


def prep(k, v, q):
    scratch = [pltpu.VMEM((T, D), BF), pltpu.SemaphoreType.DMA((3,))]
    out = (SD((T, 2 * D), BF), SD((T, G * D), BF))
    return call(prep_kernel, "prep", out, [ANY] * 3, scratch, 1 << 20, 60)(k, v, q)


def first(get_me, doc, q, far_q, kv):
    out = (SD((2 * NQ * 2 * D, R), BF), SD((NQ * AR, R), F32), TOKEN)
    kernel = functools.partial(first_kernel, get_me)
    scratch = [pltpu.VMEM((T, R), F32)] * 2
    return call(kernel, "att_first", out, [SM, VM, VM, VM], scratch, 1 << 31)(doc, q, far_q, kv)


def step(get_me, loads, items, doc, qt, st, kvs):
    most = max(x[3] for x in items) * T
    n = len(loads) * T
    scratch = (
        [pltpu.VMEM((most, R), F32)] * 2
        + [pltpu.VMEM((most, R), BF)] * 2
        + [pltpu.VMEM((n, 2 * D), BF), pltpu.VMEM((AR, n), BF)]
    )
    kernel = functools.partial(step_kernel, get_me, loads, items)
    out = (SD((len(items) * AR, R), F32), TOKEN)
    specs = [SM] + [VM] * (2 + len(kvs))
    return call(kernel, "att_step", out, specs, scratch, len(items) << 30)(doc, qt, st, *kvs)


def merge(mine, theirs, w):
    out = (SD((T, G * D), BF), SD((64, QB), F32))
    return call(merge_kernel, "att_merge", out, [VM] * 3, [], 1 << 30)(mine, theirs, w)


BOTH = lambda which, back: ((which, back), (which, back))
NEW_ITEMS = [(i, i if i < NQ else None, 0, 1) for i in range(2 * NQ)]
ENDS_LOADS = [BOTH(0, 4), ((1, 0), (0, 4))]
ENDS_ITEMS = [(i, i, i // NQ, 1) for i in range(2 * NQ)]
ONE = lambda back: [BOTH(0, back)]
ALL_ITEMS = [(i, i, 0, 1) for i in range(2 * NQ)]
THEIR_ITEMS = [(NQ + i, NQ + i, 0, 1) for i in range(NQ)]
MY_ITEMS = [(i, i, 0, 1) for i in range(NQ)]


def shards(queries, key_head_rows, values, doc_lengths, score_weight):
    ctx = lax.axis_size("ctx")
    me = functools.partial(lax.axis_index, "ctx")

    def shift(x, by):
        return lax.ppermute(x, "ctx", [(i, (i + by) % ctx) for i in range(ctx)])

    def swap(x):
        return lax.ppermute(x, "ctx", [(i, i ^ 1) for i in range(ctx)])

    kv, q = prep(key_head_rows, values, queries)
    weights = jnp.pad(score_weight.reshape(G, D), ((0, 16 - G), (0, 0)))
    back1 = shift(kv, 2)
    qt, state, token = first(me, doc_lengths, q, swap(q), kv)
    back4 = shift(after(kv, token), 8)
    back1 = after(back1, token)
    back2 = shift(back1, 2)
    state, token = step(me, ONE(1), NEW_ITEMS, doc_lengths, qt, state, [back1])
    back4 = after(back4, token)
    back3 = shift(back4, -2)
    state, _ = step(me, ENDS_LOADS, ENDS_ITEMS, doc_lengths, qt, state, [back4, kv])
    state, _ = step(me, ONE(2), ALL_ITEMS, doc_lengths, qt, state, [back2])
    theirs, _ = step(me, ONE(3), THEIR_ITEMS, doc_lengths, qt, state, [back3])
    mine, _ = step(me, ONE(3), MY_ITEMS, doc_lengths, qt, state, [back3])
    attended, part = merge(mine, swap(theirs), weights)
    parts = lax.all_to_all(part, "tp", 0, 0, tiled=True)
    score = jnp.sum(parts.reshape(8, 8, QB), axis=0)[:NQ]
    return attended, score.reshape(T)


def solution(mesh):
    return jax.shard_map(
        shards,
        mesh=mesh,
        in_specs=(P("ctx", "tp"), P("ctx", "tp"), P("ctx", "tp"), P(), P("tp")),
        out_specs=(P("ctx", "tp"), P("ctx")),
        check_vma=False,
    )
```

```python
import functools
import math

import jax
import jax.numpy as jnp
from jax import lax
from jax.experimental import pallas as pl
from jax.experimental.pallas import tpu as pltpu
from jax.sharding import PartitionSpec as P

D = 128
T = 512
QB = 128
G = 4
R = QB * G
NQ = T // QB
AR = D + 16
TOP = D + 8
NDOC = 16
BK = 256
FAR = 1 << 28
C = math.log2(math.e) / math.sqrt(D)
NEG = -1e30
F32 = jnp.float32
BF = jnp.bfloat16
SD = jax.ShapeDtypeStruct
VM = pl.BlockSpec(memory_space=pltpu.VMEM)
TOKEN = SD((16, 128), BF)
ANY = pl.BlockSpec(memory_space=pl.ANY)
SM = pl.BlockSpec(memory_space=pltpu.SMEM)


def offsets(doc_ref, index):
    start = jnp.int32(0)
    out = jnp.full(index.shape, FAR, jnp.int32)
    for d in range(NDOC):
        out = jnp.where(index == d, start, out)
        start = start + doc_ref[0, d]
    return out


def prep_kernel(k_ref, v_ref, q_ref, kv_ref, q_out, held, sems):
    values = pltpu.make_async_copy(v_ref, held, sems.at[0])
    keys = pltpu.make_async_copy(k_ref, kv_ref.at[:, :D], sems.at[1])
    queries = pltpu.make_async_copy(q_ref, q_out, sems.at[2])
    values.start()
    keys.start()
    queries.start()
    values.wait()
    for i in range(T // D):
        rows = slice(i * D, (i + 1) * D)
        kv_ref[rows, D:] = held[rows, :].T
    keys.wait()
    queries.wait()


def value_rows(kv_ref):
    blocks = [kv_ref[i * D : (i + 1) * D, D:] for i in range(T // D)]
    return jnp.concatenate(
        [jnp.concatenate(blocks, 1), jnp.ones((AR - D, T), BF)], 0
    )


def first_kernel(get_me, doc_ref, q_ref, far_q_ref, kv_ref, qt_ref, st_ref, token_ref, s0, s1):
    me = get_me()
    other = me + 1 - 2 * lax.rem(me, 2)
    ids = lax.broadcasted_iota(jnp.int32, (D, 1), 0)
    begin = offsets(doc_ref, ids)
    end = jnp.where(ids == NDOC - 1, FAR, offsets(doc_ref, ids + 1))
    va = value_rows(kv_ref)
    held = (s0, s1)
    tops = {}

    def turn(src, base, qb, row):
        pos = base + qb * QB + lax.broadcasted_iota(jnp.int32, (1, QB), 1)
        inside = (pos >= begin) & (pos < end)
        for h in range(G):
            cols = slice(h * D, (h + 1) * D)
            qt_ref[row : row + D, cols] = src[qb * QB : (qb + 1) * QB, cols].T
            qt_ref[row + D : row + 2 * D, cols] = jnp.where(inside, NEG, 0.0).astype(BF)
        return pos, jnp.sum(jnp.where(inside, begin, 0), axis=0, keepdims=True)

    def scores(qb):
        row = qb * 2 * D
        pos, start = turn(q_ref, me * T, qb, row)
        n = (qb + 1) * QB
        key = me * T + lax.broadcasted_iota(jnp.int32, (n, QB), 0)
        bias = jnp.where((key >= start) & (key <= pos), 0.0, NEG)
        s = jnp.dot(kv_ref[:n, :D], qt_ref[row : row + D, :], preferred_element_type=F32)
        s = s + jnp.concatenate([bias] * G, 1)
        held[qb % 2][:n] = s
        tops[qb] = jnp.max(s, axis=0, keepdims=True)

    token_ref[...] = jnp.zeros_like(token_ref)
    scores(0)
    for qb in range(NQ):
        if qb + 1 < NQ:
            scores(qb + 1)
        n = (qb + 1) * QB
        p = jnp.exp2((held[qb % 2][:n] - tops[qb]) * C).astype(BF)
        o = jnp.dot(va[:, :n], p, preferred_element_type=F32)
        put_state(st_ref, qb, o, tops[qb])
    for qb in range(NQ):
        turn(far_q_ref, other * T, qb, (NQ + qb) * 2 * D)


def put_state(st_ref, qb, o, top):
    st_ref[qb * AR : qb * AR + TOP, :] = o[:TOP]
    st_ref[qb * AR + TOP : (qb + 1) * AR, :] = jnp.broadcast_to(top, (AR - TOP, R))


def get_state(st_ref, qb):
    return st_ref[qb * AR : qb * AR + TOP, :], st_ref[qb * AR + TOP : qb * AR + TOP + 1, :]


def step_kernel(get_me, loads, items, doc_ref, qt_ref, st_ref, *refs):
    me = get_me()
    core = lax.rem(me, 2)
    offs = offsets(doc_ref, lax.broadcasted_iota(jnp.int32, (1, D), 1))
    kv = refs[:-8]
    out_ref, token_ref, s0, s1, p0, p1, ka, va = refs[-8:]
    held, probs = (s0, s1), (p0, p1)
    token_ref[...] = jnp.zeros_like(token_ref)

    def load(slot, which, back):
        key = (me - 2 * back) * T + lax.broadcasted_iota(jnp.int32, (T, 1), 0)
        rows = slice(slot * T, (slot + 1) * T)
        ka[rows, :D] = kv[which][:, :D]
        ka[rows, D:] = jnp.where(key < offs, 1.0, 0.0).astype(BF)
        va[:, rows] = value_rows(kv[which])

    for slot, (even, odd) in enumerate(loads):
        if even == odd:
            load(slot, *even)
        else:
            pl.when(core == 0)(functools.partial(load, slot, *even))
            pl.when(core == 1)(functools.partial(load, slot, *odd))

    top = {}
    count = len(items)
    for i in range(-1, count + 1):
        mx = o = None
        blocks = max(x[3] for x in items) * T // BK
        for j in range(blocks):
            rows = slice(j * BK, (j + 1) * BK)
            if i + 1 < count:
                qb, _, slot, _ = items[i + 1]
                s = jnp.dot(
                    ka[slot * T + j * BK : slot * T + (j + 1) * BK, :],
                    qt_ref[qb * 2 * D : (qb + 1) * 2 * D, :],
                    preferred_element_type=F32,
                )
                held[(i + 1) % 2][rows, :] = s
                x = jnp.max(s.reshape(BK // 8, 8, R), axis=0)
                mx = x if mx is None else jnp.maximum(mx, x)
            if 0 <= i < count:
                probs[i % 2][rows, :] = jnp.exp2((held[i % 2][rows, :] - top[i]) * C).astype(BF)
            if i >= 1:
                slot = items[i - 1][2]
                x = jnp.dot(
                    va[:, slot * T + j * BK : slot * T + (j + 1) * BK],
                    probs[(i - 1) % 2][rows, :],
                    preferred_element_type=F32,
                )
                o = x if o is None else o + x
        if i + 1 < count:
            top[i + 1] = jnp.max(mx, axis=0, keepdims=True)
            if items[i + 1][1] is not None:
                top[i + 1] = jnp.maximum(top[i + 1], get_state(st_ref, items[i + 1][1])[1])
        if i >= 1:
            o = o[:TOP]
            if items[i - 1][1] is not None:
                before, prior = get_state(st_ref, items[i - 1][1])
                o = before * jnp.exp2((prior - top[i - 1]) * C) + o
            put_state(out_ref, i - 1, o, top[i - 1])


def merge_kernel(mine_ref, theirs_ref, w_ref, out_ref, part_ref):
    part_ref[...] = jnp.zeros_like(part_ref)
    for qb in range(NQ):
        a, a_top = get_state(mine_ref, qb)
        b, b_top = get_state(theirs_ref, qb)
        top = jnp.maximum(a_top, b_top)
        o = a * jnp.exp2((a_top - top) * C) + b * jnp.exp2((b_top - top) * C)
        ob = (o[:D] * (1.0 / o[D : D + 1])).astype(BF)
        for h in range(G):
            cols = slice(h * D, (h + 1) * D)
            out_ref[qb * QB : (qb + 1) * QB, cols] = ob[:, cols].T
        heads = jnp.dot(w_ref[...], ob, preferred_element_type=F32)
        score = sum(heads[h : h + 1, h * D : (h + 1) * D] for h in range(G))
        for z in range(8):
            part_ref[z * 8 + qb : z * 8 + qb + 1, :] = score


def call(kernel, name, out, specs, scratch, flops, vmem=36):
    return pl.pallas_call(
        kernel,
        out_shape=out,
        in_specs=specs,
        out_specs=jax.tree.map(lambda _: VM, out),
        scratch_shapes=scratch,
        name=name,
        cost_estimate=pl.CostEstimate(flops=flops, bytes_accessed=1 << 20, transcendentals=0),
        compiler_params=pltpu.CompilerParams(vmem_limit_bytes=vmem << 20),
    )


def after_kernel(x_ref, token_ref, out_ref):
    out_ref[...] = x_ref[...]


def after(x, token):
    return call(after_kernel, "after", SD(x.shape, x.dtype), [VM, VM], [], 1 << 20)(x, token)


def pick_kernel(get_me, rows, a_ref, b_ref, token_ref, out_ref, copy_ref):
    row = lax.rem(lax.div(get_me(), 2), 4)
    hit = functools.reduce(jnp.logical_or, [row == r for r in rows])
    copy_ref[...] = b_ref[...]

    @pl.when(hit)
    def _():
        out_ref[...] = a_ref[...]

    @pl.when(jnp.logical_not(hit))
    def _():
        out_ref[...] = b_ref[...]


def pick(get_me, rows, a, b, token):
    kernel = functools.partial(pick_kernel, get_me, rows)
    out = (SD(a.shape, a.dtype), SD(b.shape, b.dtype))
    return call(kernel, "pick", out, [VM] * 3, [], 1 << 20)(a, b, token)


def prep(k, v, q):
    scratch = [pltpu.VMEM((T, D), BF), pltpu.SemaphoreType.DMA((3,))]
    out = (SD((T, 2 * D), BF), SD((T, G * D), BF))
    return call(prep_kernel, "prep", out, [ANY] * 3, scratch, 1 << 20, 60)(k, v, q)


def first(get_me, doc, q, far_q, kv):
    out = (SD((2 * NQ * 2 * D, R), BF), SD((NQ * AR, R), F32), TOKEN)
    kernel = functools.partial(first_kernel, get_me)
    scratch = [pltpu.VMEM((T, R), F32)] * 2
    return call(kernel, "att_first", out, [SM, VM, VM, VM], scratch, 1 << 31)(doc, q, far_q, kv)


def step(get_me, loads, items, doc, qt, st, kvs):
    most = max(x[3] for x in items) * T
    n = len(loads) * T
    scratch = (
        [pltpu.VMEM((most, R), F32)] * 2
        + [pltpu.VMEM((most, R), BF)] * 2
        + [pltpu.VMEM((n, 2 * D), BF), pltpu.VMEM((AR, n), BF)]
    )
    kernel = functools.partial(step_kernel, get_me, loads, items)
    out = (SD((len(items) * AR, R), F32), TOKEN)
    specs = [SM] + [VM] * (2 + len(kvs))
    return call(kernel, "att_step", out, specs, scratch, len(items) << 30)(doc, qt, st, *kvs)


def merge(mine, theirs, w):
    out = (SD((T, G * D), BF), SD((64, QB), F32))
    return call(merge_kernel, "att_merge", out, [VM] * 3, [], 1 << 30)(mine, theirs, w)


BOTH = lambda which, back: ((which, back), (which, back))
NEW_ITEMS = [(i, i if i < NQ else None, 0, 1) for i in range(2 * NQ)]
ENDS_LOADS = [BOTH(0, 4), ((1, 0), (0, 4))]
ENDS_ITEMS = [(i, i, i // NQ, 1) for i in range(2 * NQ)]
NEW_ENDS = [(i, i if i < NQ else None, i // NQ, 1) for i in range(2 * NQ)]
ONE = lambda back: [BOTH(0, back)]
ALL_ITEMS = [(i, i, 0, 1) for i in range(2 * NQ)]
THEIR_ITEMS = [(NQ + i, NQ + i, 0, 1) for i in range(NQ)]
MY_ITEMS = [(i, i, 0, 1) for i in range(NQ)]


def shards(queries, key_head_rows, values, doc_lengths, score_weight):
    ctx = lax.axis_size("ctx")
    me = functools.partial(lax.axis_index, "ctx")

    def shift(x, by):
        return lax.ppermute(x, "ctx", [(i, (i + by) % ctx) for i in range(ctx)])

    def swap(x):
        return lax.ppermute(x, "ctx", [(i, i ^ 1) for i in range(ctx)])

    def ring(x, row_of):
        pairs = [(x_ * 8 + y * 2 + c, x_ * 8 + row_of(y) * 2 + c) for x_ in range(ctx // 8) for y in range(4) for c in range(2)]
        return lax.ppermute(x, "ctx", pairs)

    kv, q = prep(key_head_rows, values, queries)
    weights = jnp.pad(score_weight.reshape(G, D), ((0, 16 - G), (0, 0)))
    back1 = shift(kv, 2)
    qt, state, token = first(me, doc_lengths, q, swap(q), kv)
    back4 = shift(after(kv, token), 8)
    back1 = after(back1, token)
    back2 = shift(back1, 2)
    state, token = step(me, ONE(1), NEW_ITEMS, doc_lengths, qt, state, [back1])
    down, back4 = pick(me, [0], kv, back4, token)
    back3 = ring(down, lambda y: (y + 3) % 4)
    state, _ = step(me, ENDS_LOADS, ENDS_ITEMS, doc_lengths, qt, state, [back4, kv])
    state, _ = step(me, ONE(2), ALL_ITEMS, doc_lengths, qt, state, [back2])
    theirs, _ = step(me, ONE(3), THEIR_ITEMS, doc_lengths, qt, state, [back3])
    mine, _ = step(me, ONE(3), MY_ITEMS, doc_lengths, qt, state, [back3])
    attended, part = merge(mine, swap(theirs), weights)
    parts = lax.all_to_all(part, "tp", 0, 0, tiled=True)
    score = jnp.sum(parts.reshape(8, 8, QB), axis=0)[:NQ]
    return attended, score.reshape(T)


def solution(mesh):
    return jax.shard_map(
        shards,
        mesh=mesh,
        in_specs=(P("ctx", "tp"), P("ctx", "tp"), P("ctx", "tp"), P(), P("tp")),
        out_specs=(P("ctx", "tp"), P("ctx")),
        check_vma=False,
    )
```

```python
import functools
import math

import jax
import jax.numpy as jnp
from jax import lax
from jax.experimental import pallas as pl
from jax.experimental.pallas import tpu as pltpu
from jax.sharding import PartitionSpec as P

D = 128
T = 512
QB = 128
G = 4
R = QB * G
NQ = T // QB
AR = D + 16
TOP = D + 8
NDOC = 16
BK = 256
FAR = 1 << 28
C = math.log2(math.e) / math.sqrt(D)
NEG = -1e30
F32 = jnp.float32
BF = jnp.bfloat16
SD = jax.ShapeDtypeStruct
VM = pl.BlockSpec(memory_space=pltpu.VMEM)
TOKEN = SD((16, 128), BF)
ANY = pl.BlockSpec(memory_space=pl.ANY)
SM = pl.BlockSpec(memory_space=pltpu.SMEM)


def offsets(doc_ref, index):
    start = jnp.int32(0)
    out = jnp.full(index.shape, FAR, jnp.int32)
    for d in range(NDOC):
        out = jnp.where(index == d, start, out)
        start = start + doc_ref[0, d]
    return out


def prep_kernel(k_ref, v_ref, kv_ref, held, sems):
    values = pltpu.make_async_copy(v_ref, held, sems.at[0])
    keys = pltpu.make_async_copy(k_ref, kv_ref.at[:, :D], sems.at[1])
    values.start()
    keys.start()
    values.wait()
    for i in range(T // D):
        rows = slice(i * D, (i + 1) * D)
        kv_ref[rows, D:] = held[rows, :].T
    keys.wait()


def value_rows(kv_ref):
    blocks = [kv_ref[i * D : (i + 1) * D, D:] for i in range(T // D)]
    return jnp.concatenate(
        [jnp.concatenate(blocks, 1), jnp.ones((AR - D, T), BF)], 0
    )


def first_kernel(get_me, doc_ref, q_ref, far_q_ref, kv_ref, qt_ref, st_ref, token_ref, s0, s1):
    me = get_me()
    other = me + 1 - 2 * lax.rem(me, 2)
    ids = lax.broadcasted_iota(jnp.int32, (D, 1), 0)
    begin = offsets(doc_ref, ids)
    end = jnp.where(ids == NDOC - 1, FAR, offsets(doc_ref, ids + 1))
    va = value_rows(kv_ref)
    held = (s0, s1)
    tops = {}

    def turn(src, base, qb, row):
        pos = base + qb * QB + lax.broadcasted_iota(jnp.int32, (1, QB), 1)
        inside = (pos >= begin) & (pos < end)
        for h in range(G):
            cols = slice(h * D, (h + 1) * D)
            qt_ref[row : row + D, cols] = src[qb * QB : (qb + 1) * QB, cols].T
            qt_ref[row + D : row + 2 * D, cols] = jnp.where(inside, NEG, 0.0).astype(BF)
        return pos, jnp.sum(jnp.where(inside, begin, 0), axis=0, keepdims=True)

    def scores(qb):
        row = qb * 2 * D
        pos, start = turn(q_ref, me * T, qb, row)
        n = (qb + 1) * QB
        key = me * T + lax.broadcasted_iota(jnp.int32, (n, QB), 0)
        bias = jnp.where((key >= start) & (key <= pos), 0.0, NEG)
        s = jnp.dot(kv_ref[:n, :D], qt_ref[row : row + D, :], preferred_element_type=F32)
        s = s + jnp.concatenate([bias] * G, 1)
        held[qb % 2][:n] = s
        tops[qb] = jnp.max(s, axis=0, keepdims=True)

    token_ref[...] = jnp.zeros_like(token_ref)
    scores(0)
    for qb in range(NQ):
        if qb + 1 < NQ:
            scores(qb + 1)
        n = (qb + 1) * QB
        p = jnp.exp2((held[qb % 2][:n] - tops[qb]) * C).astype(BF)
        o = jnp.dot(va[:, :n], p, preferred_element_type=F32)
        put_state(st_ref, qb, o, tops[qb])
    for qb in range(NQ):
        turn(far_q_ref, other * T, qb, (NQ + qb) * 2 * D)


def put_state(st_ref, qb, o, top):
    st_ref[qb * AR : qb * AR + TOP, :] = o[:TOP]
    st_ref[qb * AR + TOP : (qb + 1) * AR, :] = jnp.broadcast_to(top, (AR - TOP, R))


def get_state(st_ref, qb):
    return st_ref[qb * AR : qb * AR + TOP, :], st_ref[qb * AR + TOP : qb * AR + TOP + 1, :]


def step_kernel(get_me, loads, items, doc_ref, qt_ref, st_ref, *refs):
    me = get_me()
    core = lax.rem(me, 2)
    offs = offsets(doc_ref, lax.broadcasted_iota(jnp.int32, (1, D), 1))
    kv = refs[:-8]
    out_ref, token_ref, s0, s1, p0, p1, ka, va = refs[-8:]
    held, probs = (s0, s1), (p0, p1)
    token_ref[...] = jnp.zeros_like(token_ref)

    def load(slot, which, back):
        key = (me - 2 * back) * T + lax.broadcasted_iota(jnp.int32, (T, 1), 0)
        rows = slice(slot * T, (slot + 1) * T)
        ka[rows, :D] = kv[which][:, :D]
        ka[rows, D:] = jnp.where(key < offs, 1.0, 0.0).astype(BF)
        va[:, rows] = value_rows(kv[which])

    for slot, (even, odd) in enumerate(loads):
        if even == odd:
            load(slot, *even)
        else:
            pl.when(core == 0)(functools.partial(load, slot, *even))
            pl.when(core == 1)(functools.partial(load, slot, *odd))

    top = {}
    count = len(items)
    for i in range(-1, count + 1):
        mx = o = None
        blocks = max(x[3] for x in items) * T // BK
        for j in range(blocks):
            rows = slice(j * BK, (j + 1) * BK)
            if i + 1 < count:
                qb, _, slot, _ = items[i + 1]
                s = jnp.dot(
                    ka[slot * T + j * BK : slot * T + (j + 1) * BK, :],
                    qt_ref[qb * 2 * D : (qb + 1) * 2 * D, :],
                    preferred_element_type=F32,
                )
                held[(i + 1) % 2][rows, :] = s
                x = jnp.max(s.reshape(BK // 8, 8, R), axis=0)
                mx = x if mx is None else jnp.maximum(mx, x)
            if 0 <= i < count:
                probs[i % 2][rows, :] = jnp.exp2((held[i % 2][rows, :] - top[i]) * C).astype(BF)
            if i >= 1:
                slot = items[i - 1][2]
                x = jnp.dot(
                    va[:, slot * T + j * BK : slot * T + (j + 1) * BK],
                    probs[(i - 1) % 2][rows, :],
                    preferred_element_type=F32,
                )
                o = x if o is None else o + x
        if i + 1 < count:
            top[i + 1] = jnp.max(mx, axis=0, keepdims=True)
            if items[i + 1][1] is not None:
                top[i + 1] = jnp.maximum(top[i + 1], get_state(st_ref, items[i + 1][1])[1])
        if i >= 1:
            o = o[:TOP]
            if items[i - 1][1] is not None:
                before, prior = get_state(st_ref, items[i - 1][1])
                o = before * jnp.exp2((prior - top[i - 1]) * C) + o
            put_state(out_ref, i - 1, o, top[i - 1])


def merge_kernel(mine_ref, theirs_ref, w_ref, out_ref, part_ref):
    for qb in range(NQ):
        a, a_top = get_state(mine_ref, qb)
        b, b_top = get_state(theirs_ref, qb)
        top = jnp.maximum(a_top, b_top)
        o = a * jnp.exp2((a_top - top) * C) + b * jnp.exp2((b_top - top) * C)
        ob = (o[:D] * (1.0 / o[D : D + 1])).astype(BF)
        for h in range(G):
            cols = slice(h * D, (h + 1) * D)
            out_ref[qb * QB : (qb + 1) * QB, cols] = ob[:, cols].T
        heads = jnp.dot(w_ref[...], ob, preferred_element_type=F32)
        score = sum(heads[h : h + 1, h * D : (h + 1) * D] for h in range(G))
        for z in range(8):
            part_ref[z * NQ + qb : z * NQ + qb + 1, :] = score


def call(kernel, name, out, specs, scratch, flops, vmem=36):
    return pl.pallas_call(
        kernel,
        out_shape=out,
        in_specs=specs,
        out_specs=jax.tree.map(lambda _: VM, out),
        scratch_shapes=scratch,
        name=name,
        cost_estimate=pl.CostEstimate(flops=flops, bytes_accessed=1 << 20, transcendentals=0),
        compiler_params=pltpu.CompilerParams(vmem_limit_bytes=vmem << 20),
    )


def after_kernel(x_ref, token_ref, out_ref):
    out_ref[...] = x_ref[...]


def after(x, token):
    return call(after_kernel, "after", SD(x.shape, x.dtype), [VM, VM], [], 1 << 20)(x, token)


def pick_kernel(get_me, rows, a_ref, b_ref, token_ref, out_ref, copy_ref):
    row = lax.rem(lax.div(get_me(), 2), 4)
    hit = functools.reduce(jnp.logical_or, [row == r for r in rows])
    copy_ref[...] = b_ref[...]

    @pl.when(hit)
    def _():
        out_ref[...] = a_ref[...]

    @pl.when(jnp.logical_not(hit))
    def _():
        out_ref[...] = b_ref[...]


def pick(get_me, rows, a, b, token):
    kernel = functools.partial(pick_kernel, get_me, rows)
    out = (SD(a.shape, a.dtype), SD(b.shape, b.dtype))
    return call(kernel, "pick", out, [VM] * 3, [], 1 << 20)(a, b, token)


def prep(k, v):
    scratch = [pltpu.VMEM((T, D), BF), pltpu.SemaphoreType.DMA((2,))]
    return call(prep_kernel, "prep", SD((T, 2 * D), BF), [ANY] * 2, scratch, 1 << 20, 60)(k, v)


def first(get_me, doc, q, far_q, kv):
    out = (SD((2 * NQ * 2 * D, R), BF), SD((NQ * AR, R), F32), TOKEN)
    kernel = functools.partial(first_kernel, get_me)
    scratch = [pltpu.VMEM((T, R), F32)] * 2
    return call(kernel, "att_first", out, [SM, VM, VM, VM], scratch, 1 << 31)(doc, q, far_q, kv)


def step(get_me, loads, items, doc, qt, st, kvs):
    most = max(x[3] for x in items) * T
    n = len(loads) * T
    scratch = (
        [pltpu.VMEM((most, R), F32)] * 2
        + [pltpu.VMEM((most, R), BF)] * 2
        + [pltpu.VMEM((n, 2 * D), BF), pltpu.VMEM((AR, n), BF)]
    )
    kernel = functools.partial(step_kernel, get_me, loads, items)
    out = (SD((len(items) * AR, R), F32), TOKEN)
    specs = [SM] + [VM] * (2 + len(kvs))
    return call(kernel, "att_step", out, specs, scratch, len(items) << 30)(doc, qt, st, *kvs)


def merge(mine, theirs, w):
    out = (SD((T, G * D), BF), SD((8 * NQ, QB), F32))
    return call(merge_kernel, "att_merge", out, [VM] * 3, [], 1 << 30)(mine, theirs, w)


BOTH = lambda which, back: ((which, back), (which, back))
NEW_ITEMS = [(i, i if i < NQ else None, 0, 1) for i in range(2 * NQ)]
ENDS_LOADS = [BOTH(0, 4), ((1, 0), (0, 4))]
ENDS_ITEMS = [(i, i, i // NQ, 1) for i in range(2 * NQ)]
NEW_ENDS = [(i, i if i < NQ else None, i // NQ, 1) for i in range(2 * NQ)]
ONE = lambda back: [BOTH(0, back)]
ALL_ITEMS = [(i, i, 0, 1) for i in range(2 * NQ)]
THEIR_ITEMS = [(NQ + i, NQ + i, 0, 1) for i in range(NQ)]
MY_ITEMS = [(i, i, 0, 1) for i in range(NQ)]


def shards(queries, key_head_rows, values, doc_lengths, score_weight):
    ctx = lax.axis_size("ctx")
    me = functools.partial(lax.axis_index, "ctx")

    def shift(x, by):
        return lax.ppermute(x, "ctx", [(i, (i + by) % ctx) for i in range(ctx)])

    def swap(x):
        return lax.ppermute(x, "ctx", [(i, i ^ 1) for i in range(ctx)])

    def ring(x, row_of):
        pairs = [(x_ * 8 + y * 2 + c, x_ * 8 + row_of(y) * 2 + c) for x_ in range(ctx // 8) for y in range(4) for c in range(2)]
        return lax.ppermute(x, "ctx", pairs)

    kv = prep(key_head_rows, values)
    weights = jnp.pad(score_weight.reshape(G, D), ((0, 16 - G), (0, 0)))
    back1 = shift(kv, 2)
    qt, state, token = first(me, doc_lengths, queries, swap(queries), kv)
    back4 = shift(after(kv, token), 8)
    back1 = after(back1, token)
    back2 = shift(back1, 2)
    state, token = step(me, ONE(1), NEW_ITEMS, doc_lengths, qt, state, [back1])
    down, back4 = pick(me, [0], kv, back4, token)
    back3 = ring(down, lambda y: (y + 3) % 4)
    state, _ = step(me, ENDS_LOADS, ENDS_ITEMS, doc_lengths, qt, state, [back4, kv])
    state, _ = step(me, ONE(2), ALL_ITEMS, doc_lengths, qt, state, [back2])
    theirs, _ = step(me, ONE(3), THEIR_ITEMS, doc_lengths, qt, state, [back3])
    mine, _ = step(me, ONE(3), MY_ITEMS, doc_lengths, qt, state, [back3])
    attended, part = merge(mine, swap(theirs), weights)
    parts = lax.all_to_all(part, "tp", 0, 0, tiled=True)
    score = jnp.sum(parts.reshape(8, NQ, QB), axis=0)
    return attended, score.reshape(T)


def solution(mesh):
    return jax.shard_map(
        shards,
        mesh=mesh,
        in_specs=(P("ctx", "tp"), P("ctx", "tp"), P("ctx", "tp"), P(), P("tp")),
        out_specs=(P("ctx", "tp"), P("ctx")),
        check_vma=False,
    )
```
